32 devices in a mesh: mem: 8 (over z, x), lev: 4 (over y, core).
Axes of the slice: x: 2, y: 2, z: 4, core: 2. Of those that a mesh axis runs over, the one named last changes fastest.
Arguments:
- background_trajectories: float32 [1024, 8, 8, 128], P('mem', None, 'lev')
- linear_sensor_mapping: float32 [8, 128, 128], P('lev'), may hold values from -0.1875 to 0.1875
- jittered_sensor_values: float32 [1024, 8, 128], P('mem'), may hold values from -6 to 6
- residual_precision_tiles: float32 [8, 128, 128], replicated, as said below
- measurement_tile_table: int32 [8, 16], replicated, may hold values from 0 to 7, as said below
- holder_rank: int32 [8], replicated, may hold values from 0 to 7, as said below
Outputs:
- analysis: float32 [1024, 16, 8, 128], P(None, 'mem', 'lev')
The draws below stay inside these ranges and needn't reach their ends.
Inputs may be any that keep to these rules, and one draw needn't show every extreme that they name: `measurement_tile_table`: entry (b, q) lies within 12 blocks of b on the cycle of blocks; a row's entries are distinct where 8 >= 25. `holder_rank`: each index owns at most 2 blocks, and some index owns exactly 2. `residual_precision_tiles`: symmetric.
All inputs are finite; a program needn't handle non-finite values.
Results may differ from the reference program's by a relative error of at most 0.0094.
Values may be sent and summed in bfloat16 or wider, within the bound.
A program may use at most 128 MiB of HBM per device.

```python
import jax
import jax.numpy as jnp
from jax import lax

MEMBER_COUNT = 1024
LAYER_BANDS = 8
TILE_SITES = 128
OBS = 128
LIST = 16
REACH = 12
NB = 8
CAP = 2
SLOTS = 16


def draw_background_trajectories(key, part):
    key = jax.random.fold_in(key, 11)
    key_base, key_noise = jax.random.split(key, 2)
    base_field = jax.random.uniform(key_base, (NB, LAYER_BANDS, TILE_SITES), jnp.float32, -2.0, 2.0)
    member_noise = jax.random.normal(key_noise, (MEMBER_COUNT, NB, LAYER_BANDS, TILE_SITES), jnp.float32)
    return base_field[None] + member_noise


def draw_residual_precision_tiles(key, part):
    key = jax.random.fold_in(key, 7)
    key_off, key_diag = jax.random.split(key)
    raw_part = jax.random.normal(key_off, (NB, OBS, OBS), jnp.float32)
    diagonal = jax.random.uniform(key_diag, (NB, OBS), jnp.float32, 1.2, 2.4)
    symmetric = (raw_part + jnp.swapaxes(raw_part, 1, 2)) * (0.04 / 1.4142135)
    identity = jnp.eye(OBS, dtype=jnp.float32)
    return symmetric * (1.0 - identity) + diagonal[:, :, None] * identity


def draw_measurement_tile_table(key, part):
    key = jax.random.fold_in(key, 3)
    choices_count = 2 * REACH + 1
    scores = jax.random.randint(key, (NB, choices_count), 0, 1048576)
    distinct = scores * choices_count + jnp.arange(choices_count, dtype=jnp.int32)[None, :]
    order = jnp.argsort(distinct, axis=1, stable=True)[:, :LIST].astype(jnp.int32)
    offsets = order - REACH
    blocks = jnp.arange(NB, dtype=jnp.int32)
    return jnp.mod(blocks[:, None] + offsets, NB).astype(jnp.int32)


def draw_holder_rank(key, part):
    key = jax.random.fold_in(key, 5)
    key_full, key_perm, key_assign = jax.random.split(key, 3)
    fullest = jax.random.randint(key_full, (), 0, SLOTS // CAP)
    shuffled = jax.random.permutation(key_perm, SLOTS).astype(jnp.int32)
    slot_ids = jnp.arange(SLOTS, dtype=jnp.int32)
    priority = jnp.where(slot_ids // CAP == fullest, -1 - slot_ids, shuffled)
    picked = jnp.argsort(priority, stable=True)[:NB]
    owners = (picked // CAP).astype(jnp.int32)
    return jax.random.permutation(key_assign, owners).astype(jnp.int32)


def steps_of(stream_key, dims, shards, smallest, top_value):
    level, own = 1.0, jax.random.fold_in(stream_key, 6)
    for axis_at, parts in shards:
        heights = jnp.exp(jax.random.uniform(jax.random.fold_in(own, axis_at), (parts,), jnp.float32, smallest / len(shards), top_value / len(shards)))
        level = level * jnp.repeat(heights, dims[axis_at] // parts).reshape([-1 if axis == axis_at else 1 for axis in range(len(dims))])
    return level


def normal_values(own_key, extent, width, bound, pieces=(), kind=jnp.bfloat16):
    values = jax.random.normal(own_key, extent, jnp.float32) * width
    if len(pieces) > 0:
        values = steps_of(own_key, extent, pieces, -0.22, 0.18) * values
    return jnp.clip(values, min=-bound, max=bound).astype(kind)


def setup_inputs(seed: int = 0) -> dict:
    streams_of = jax.random.split(jax.random.key(seed), 7)
    return {
        "background_trajectories": draw_background_trajectories(jax.random.fold_in(streams_of[6], 71), 0),
        "linear_sensor_mapping": normal_values(streams_of[1], (LAYER_BANDS, TILE_SITES, OBS), (LAYER_BANDS * TILE_SITES) ** -0.5, 0.1875, ((0, 4),), jnp.float32),
        "jittered_sensor_values": normal_values(streams_of[2], (MEMBER_COUNT, NB, OBS), 1.0, 6.0, ((0, 8),), jnp.float32),
        "residual_precision_tiles": draw_residual_precision_tiles(jax.random.fold_in(streams_of[6], 71), 0),
        "measurement_tile_table": draw_measurement_tile_table(jax.random.fold_in(streams_of[6], 71), 0),
        "holder_rank": draw_holder_rank(jax.random.fold_in(streams_of[6], 71), 0),
    }


def slot_table(holder_rank):
    blocks = jnp.arange(NB, dtype=jnp.int32)
    shared_owner = holder_rank[:, None] == holder_rank[None, :]
    earlier = blocks[None, :] < blocks[:, None]
    order_rank = jnp.sum((shared_owner & earlier).astype(jnp.int32), axis=1).astype(jnp.int32)
    return (holder_rank * CAP + order_rank).astype(jnp.int32)


def taper_table(measurement_tile_table):
    blocks = jnp.arange(NB, dtype=jnp.int32)
    offsets_abs = jnp.abs(blocks[:, None] - measurement_tile_table)
    cycle_gap = jnp.minimum(offsets_abs, NB - offsets_abs).astype(jnp.float32)
    scaled = 2.0 * cycle_gap / REACH
    return 1.0 / (1.0 + scaled * scaled)


def reference(background_trajectories, linear_sensor_mapping, jittered_sensor_values, residual_precision_tiles, measurement_tile_table, holder_rank):
    largest_ordering_label = lax.Precision.HIGHEST
    background_values_mapped = jnp.einsum("vhsg,sgl->vhl", background_trajectories, linear_sensor_mapping, precision=largest_ordering_label)
    departure = jittered_sensor_values - background_values_mapped
    weighted = jnp.einsum("mbo,bop->mbp", departure, residual_precision_tiles, precision=largest_ordering_label).astype(jnp.bfloat16)
    background_halfway_piece = background_values_mapped.astype(jnp.bfloat16).astype(jnp.float32)
    mean_pred = jnp.mean(background_halfway_piece, axis=0)
    pred_pert = (background_halfway_piece - mean_pred).astype(jnp.bfloat16)
    taper_weight = taper_table(measurement_tile_table)

    def update_block(site_tile):
        listed_blocks = measurement_tile_table[site_tile]
        pred_cols = jnp.take(pred_pert, listed_blocks, axis=1).reshape(MEMBER_COUNT, LIST * OBS).astype(jnp.float32)
        weight_cols = jnp.take(weighted, listed_blocks, axis=1).reshape(MEMBER_COUNT, LIST * OBS).astype(jnp.float32)
        tile_vector = lax.dynamic_index_in_dim(background_trajectories, site_tile, 1, keepdims=False).reshape(MEMBER_COUNT, LAYER_BANDS * TILE_SITES)
        state_half = tile_vector.astype(jnp.bfloat16).astype(jnp.float32)
        covariance = lax.dot_general(state_half, pred_cols, (((0,), (0,)), ((), ())))
        column_scale = jnp.repeat(taper_weight[site_tile], OBS) / (MEMBER_COUNT - 1)
        covariance = (covariance * column_scale[None, :]).astype(jnp.bfloat16).astype(jnp.float32)
        increment = jnp.dot(weight_cols, covariance.T)
        return tile_vector + increment

    analysed = lax.map(update_block, jnp.arange(NB, dtype=jnp.int32))
    analysed = jnp.transpose(analysed.reshape(NB, MEMBER_COUNT, LAYER_BANDS, TILE_SITES), (1, 0, 2, 3))
    slot_of_block = slot_table(holder_rank)
    return jnp.zeros((MEMBER_COUNT, SLOTS, LAYER_BANDS, TILE_SITES), jnp.float32).at[:, slot_of_block].set(analysed)
```

```python
import functools

import jax
import jax.numpy as jnp
from jax import lax
from jax.experimental import pallas as pl
from jax.experimental.pallas import tpu as pltpu
from jax.sharding import PartitionSpec as P

REACH = 12
CAP = 2
MESH = pl.DeviceIdType.MESH
EXACT = lax.Precision.HIGHEST


def exchange(
    mem, lev,
    tile_ref, live_ref, bg_ref, map_ref, sensed_ref, precision_ref,
    pw_ref, st_ref,
    half, outgoing, part, arrived,
    part_send, part_recv, state_send, state_recv, mem_send, mem_recv,
    y_send, y_recv, core_send, core_recv,
):
    me, lv = lax.axis_index("mem"), lax.axis_index("lev")
    blocks, members = half.shape[0], half.shape[1]
    layers = map_ref.shape[0]
    rows = members // lev
    mem_peers = [lax.rem(me + d, mem) for d in range(1, mem)]
    lev_peers = [lax.rem(lv + d, lev) for d in range(1, lev)]
    core = lv + 1 - 2 * lax.rem(lv, 2)
    across = lax.rem(lv + 2, lev)

    barrier = pltpu.get_barrier_semaphore()
    for k in mem_peers:
        pl.semaphore_signal(barrier, inc=1, device_id=(k, lv), device_id_type=MESH)
    for k in lev_peers:
        pl.semaphore_signal(barrier, inc=1, device_id=(me, k), device_id_type=MESH)

    for b in range(blocks):
        total = None
        for h in range(layers):
            piece = bg_ref[pl.ds(b * layers + h, members, stride=blocks * layers), :]
            half[b, :, h * 128:(h + 1) * 128] = piece.astype(jnp.bfloat16)
            term = jnp.dot(piece, map_ref[h], precision=EXACT, preferred_element_type=jnp.float32)
            total = term if total is None else total + term
        for q in range(lev):
            part[q, b] = total[q * rows:(q + 1) * rows]

    pl.semaphore_wait(barrier, mem - 1 + lev - 1)

    copies = []
    part_copies = []
    for d in range(1, lev):
        to = lev_peers[d - 1]
        c = pltpu.make_async_remote_copy(
            part.at[to], arrived.at[d], part_send.at[d], part_recv.at[d],
            device_id=(me, to), device_id_type=MESH)
        c.start()
        part_copies.append(c)

    state_copies = []
    for d in range(1, mem):
        to = mem_peers[d - 1]
        for c in range(CAP):
            slot = to * CAP + c
            outgoing[d, c] = half[tile_ref[slot]] * live_ref[slot].astype(jnp.bfloat16)
        c = pltpu.make_async_remote_copy(
            outgoing.at[d], st_ref.at[me], state_send.at[d], state_recv.at[d],
            device_id=(to, lv), device_id_type=MESH)
        c.start()
        state_copies.append(c)
    for c in range(CAP):
        slot = me * CAP + c
        st_ref[me, c] = half[tile_ref[slot]] * live_ref[slot].astype(jnp.bfloat16)

    for c in part_copies:
        c.wait_recv()
    for b in range(blocks):
        pred = part[lv, b]
        for d in range(1, lev):
            pred = pred + arrived[d, b]
        pw_ref[me, lv, 0, b] = pred.astype(jnp.bfloat16)
        gap = sensed_ref[pl.ds(lv * rows * blocks + b, rows, stride=blocks), :] - pred
        pw_ref[me, lv, 1, b] = jnp.dot(
            gap, precision_ref[b], precision=EXACT, preferred_element_type=jnp.float32
        ).astype(jnp.bfloat16)

    def pass_on(owner, quarter, send, recv, to):
        return pltpu.make_async_remote_copy(
            pw_ref.at[owner, quarter], pw_ref.at[owner, quarter], send, recv,
            device_id=to, device_id_type=MESH)

    mem_copies = []
    for d in range(1, mem):
        c = pass_on(me, lv, mem_send.at[d], mem_recv.at[d], (mem_peers[d - 1], lv))
        c.start()
        mem_copies.append(c)
    y_copies, core_copies = [], []
    for d in range(mem):
        source = lax.rem(me + mem - d, mem)
        if d > 0:
            pltpu.make_async_remote_copy(
                pw_ref.at[source, lv], pw_ref.at[source, lv], mem_send.at[d], mem_recv.at[d],
                device_id=(source, lv), device_id_type=MESH).wait_recv()
        c = pass_on(source, lv, y_send.at[d], y_recv.at[d], (me, across))
        c.start()
        y_copies.append(c)
        c = pass_on(source, lv, core_send.at[0, d], core_recv.at[0, d], (me, core))
        c.start()
        core_copies.append(c)
    for d in range(mem):
        source = lax.rem(me + mem - d, mem)
        pass_on(source, across, y_send.at[d], y_recv.at[d], (me, across)).wait_recv()
        c = pass_on(source, across, core_send.at[1, d], core_recv.at[1, d], (me, core))
        c.start()
        core_copies.append(c)
    other = lax.rem(core + 2, lev)
    for d in range(mem):
        source = lax.rem(me + mem - d, mem)
        pass_on(source, core, core_send.at[0, d], core_recv.at[0, d], (me, core)).wait_recv()
        pass_on(source, other, core_send.at[1, d], core_recv.at[1, d], (me, core)).wait_recv()
    for d in range(1, mem):
        source = lax.rem(me + mem - d, mem)
        pltpu.make_async_remote_copy(
            outgoing.at[d], st_ref.at[source], state_send.at[d], state_recv.at[d],
            device_id=(source, lv), device_id_type=MESH).wait_recv()
    for c in part_copies + state_copies + mem_copies + y_copies + core_copies:
        c.wait_send()


def analyse(scale_ref, pw_ref, st_ref, out_ref, covariance):
    mem, lev, _, blocks, rows, obs = pw_ref.shape
    capacity, members, width = st_ref.shape[1:]
    total = mem * members

    @pl.loop(0, blocks)
    def _(b):
        pred = pw_ref[:, :, 0, b].reshape(total, obs).astype(jnp.float32)
        mean = jnp.sum(pred, axis=0, keepdims=True) * (1.0 / total)
        pert = (pred - mean).astype(jnp.bfloat16)
        for c in range(capacity):
            cov = lax.dot_general(
                pert, st_ref[:, c].reshape(total, width), (((0,), (0,)), ((), ())),
                preferred_element_type=jnp.float32)
            covariance[pl.ds(pl.multiple_of(b * obs, obs), obs), c * width:(c + 1) * width] = (
                cov * scale_ref[c * blocks + b]).astype(jnp.bfloat16)

    parts = 4 if mem % 4 == 0 else mem
    chunk = mem // parts

    @pl.loop(0, parts)
    def _(r):
        owners = pl.ds(r * chunk, chunk)
        weighted = jnp.concatenate(
            [pw_ref[owners, :, 1, b].reshape(chunk * members, obs) for b in range(blocks)], axis=1)
        per_slot = width // 128
        for c in range(capacity):
            rise = jnp.dot(
                weighted, covariance[:, c * width:(c + 1) * width],
                preferred_element_type=jnp.float32)
            value = st_ref[owners, c].reshape(chunk * members, width).astype(jnp.float32) + rise
            for h in range(per_slot):
                stride = capacity * per_slot
                start = r * chunk * members * stride + c * per_slot + h
                out_ref[pl.ds(start, chunk * members, stride=stride), :] = (
                    value[:, h * 128:(h + 1) * 128])


def dense_shards(mem, lev, bg, linear_map, sensed, precision, table, holder_rank):
    members, blocks, layers, sites = bg.shape
    obs = linear_map.shape[2]
    rows = members // lev
    width = layers * sites
    me = lax.axis_index("mem")
    block_ids = jnp.arange(blocks, dtype=jnp.int32)
    same = holder_rank[:, None] == holder_rank[None, :]
    earlier = block_ids[None, :] < block_ids[:, None]
    slot_of = holder_rank * CAP + jnp.sum((same & earlier).astype(jnp.int32), axis=1)
    slot_ids = jnp.arange(mem * CAP, dtype=jnp.int32)
    matches = slot_of[None, :] == slot_ids[:, None]
    live = jnp.any(matches, axis=1).astype(jnp.float32)
    tile = jnp.sum(jnp.where(matches, block_ids[None, :], 0), axis=1)
    away = jnp.abs(block_ids[:, None] - block_ids[None, :])
    gap = 2.0 * jnp.minimum(away, blocks - away).astype(jnp.float32) / REACH
    times = jnp.sum((table[:, :, None] == block_ids[None, None, :]).astype(jnp.float32), axis=1)
    weights = times / (1.0 + gap * gap) / (mem * members - 1)
    mine = (slot_of[None, :] == (me * CAP + jnp.arange(CAP, dtype=jnp.int32))[:, None])
    scale = jnp.sum(jnp.where(mine[:, :, None], weights[None], 0.0), axis=1).reshape(-1)

    smem = pl.BlockSpec(memory_space=pltpu.SMEM)
    vmem = pl.BlockSpec(memory_space=pltpu.VMEM)
    dma = pltpu.SemaphoreType.DMA
    half = jnp.bfloat16
    pw, st = pl.pallas_call(
        functools.partial(exchange, mem, lev),
        out_shape=(
            jax.ShapeDtypeStruct((mem, lev, 2, blocks, rows, obs), half),
            jax.ShapeDtypeStruct((mem, CAP, members, width), half),
        ),
        in_specs=[smem, smem, vmem, vmem, vmem, vmem],
        out_specs=(vmem, vmem),
        scratch_shapes=[
            pltpu.VMEM((blocks, members, width), half),
            pltpu.VMEM((mem, CAP, members, width), half),
            pltpu.VMEM((lev, blocks, rows, obs), jnp.float32),
            pltpu.VMEM((lev, blocks, rows, obs), jnp.float32),
            dma((lev,)), dma((lev,)), dma((mem,)), dma((mem,)), dma((mem,)), dma((mem,)),
            dma((mem,)), dma((mem,)), dma((2, mem)), dma((2, mem)),
        ],
        compiler_params=pltpu.CompilerParams(
            collective_id=0, has_side_effects=True, vmem_limit_bytes=40 * 2**20),
        name="exchange",
    )(
        tile, live, bg.reshape(members * blocks * layers, sites), linear_map,
        sensed.reshape(members * blocks, obs), precision,
    )
    out = pl.pallas_call(
        analyse,
        out_shape=jax.ShapeDtypeStruct((mem * members * CAP * layers, sites), jnp.float32),
        in_specs=[smem, vmem, vmem],
        out_specs=vmem,
        scratch_shapes=[pltpu.VMEM((blocks * obs, CAP * width), half)],
        compiler_params=pltpu.CompilerParams(vmem_limit_bytes=40 * 2**20),
        name="analyse",
    )(scale, pw, st)
    return out.reshape(mem * members, CAP, layers, sites)


def shards(
    background_trajectories,
    linear_sensor_mapping,
    jittered_sensor_values,
    residual_precision_tiles,
    measurement_tile_table,
    holder_rank,
):
    largest_ordering_label = lax.Precision.HIGHEST
    mem_count = lax.axis_size("mem")
    my_index = lax.axis_index("mem")
    resident_realizations, tile_count, layer_count, mesh_sites = background_trajectories.shape
    obs_width = linear_sensor_mapping.shape[2]
    listed = measurement_tile_table.shape[1]
    capacity = CAP
    slot_count = mem_count * capacity
    partial_observed = jnp.einsum(
        "vhsg,sgl->vhl",
        background_trajectories,
        linear_sensor_mapping,
        precision=largest_ordering_label,
    )
    aggregated_total = lax.psum(partial_observed, "lev")
    departure = jittered_sensor_values - aggregated_total
    weighted = jnp.einsum(
        "mbo,bop->mbp", departure, residual_precision_tiles, precision=largest_ordering_label
    ).astype(jnp.bfloat16)
    background_values_mapped = aggregated_total.astype(jnp.bfloat16)
    blocks = jnp.arange(tile_count, dtype=jnp.int32)
    shared_owner = holder_rank[:, None] == holder_rank[None, :]
    earlier = blocks[None, :] < blocks[:, None]
    order_rank = jnp.sum((shared_owner & earlier).astype(jnp.int32), axis=1)
    slot_of_block = holder_rank * capacity + order_rank
    slot_ids = jnp.arange(slot_count, dtype=jnp.int32)
    matches = slot_of_block[None, :] == slot_ids[:, None]
    active_slot = jnp.any(matches, axis=1)
    tile_at_place = jnp.sum(jnp.where(matches, blocks[None, :], 0), axis=1)
    obs_index = jnp.take(measurement_tile_table, tile_at_place, axis=0)
    offsets_abs = jnp.abs(tile_at_place[:, None] - obs_index)
    cycle_gap = jnp.minimum(offsets_abs, tile_count - offsets_abs).astype(jnp.float32)
    scaled_gap = 2.0 * cycle_gap / REACH
    taper_weight = 1.0 / (1.0 + scaled_gap * scaled_gap)
    outgoing = (
        jnp.take(background_trajectories, tile_at_place, axis=1)
        * active_slot.astype(jnp.float32)[None, :, None, None]
    )
    outgoing = outgoing.reshape(
        resident_realizations, mem_count, capacity, layer_count * mesh_sites
    )
    states = lax.all_to_all(outgoing, "mem", split_axis=1, concat_axis=0, tiled=True).reshape(
        -1, capacity, layer_count * mesh_sites
    )
    total_members = states.shape[0]
    gathered = (
        lax.all_gather(background_values_mapped, "mem", axis=0, tiled=True),
        lax.all_gather(weighted, "mem", axis=0, tiled=True),
    )
    mine_index = lax.dynamic_slice_in_dim(obs_index, my_index * capacity, capacity, 0).reshape(-1)
    mine_live = lax.dynamic_slice_in_dim(active_slot, my_index * capacity, capacity, 0)
    mine_mask = jnp.repeat(mine_live, listed).astype(jnp.bfloat16)
    pred_rows = jnp.take(gathered[0], mine_index, axis=1) * mine_mask[None, :, None]
    weight_rows = jnp.take(gathered[1], mine_index, axis=1) * mine_mask[None, :, None]
    my_taper = lax.dynamic_slice_in_dim(taper_weight, my_index * capacity, capacity, 0)
    state_half = states.astype(jnp.bfloat16)
    mean_pred = jnp.mean(pred_rows, axis=0, dtype=jnp.float32)
    pred_pert = (
        (pred_rows - mean_pred)
        .astype(jnp.bfloat16)
        .reshape(total_members, capacity, listed * obs_width)
    )
    weight_cols = weight_rows.reshape(total_members, capacity, listed * obs_width)
    covariance = jnp.einsum(
        "mcx,mcy->cxy", state_half, pred_pert, preferred_element_type=jnp.float32
    )
    column_scale = jnp.repeat(my_taper, obs_width, axis=1) / (total_members - 1)
    covariance = (covariance * column_scale[:, None, :]).astype(jnp.bfloat16)
    increment = jnp.einsum(
        "mcy,cxy->mcx", weight_cols, covariance, preferred_element_type=jnp.float32
    )
    return (states + increment).reshape(total_members, capacity, layer_count, mesh_sites)


def solution(mesh):
    in_specs = (
        P("mem", None, "lev", None),
        P("lev", None, None),
        P("mem", None, None),
        P(),
        P(),
        P(),
    )
    out_specs = P(None, "mem", "lev", None)
    mem, lev = mesh.shape["mem"], mesh.shape["lev"]

    def local(bg, linear_map, sensed, precision, table, holder_rank):
        dense = bg.shape[1] <= table.shape[1] and lev == 4 and bg.shape[0] % 64 == 0
        body = functools.partial(dense_shards, mem, lev) if dense else shards
        return body(bg, linear_map, sensed, precision, table, holder_rank)

    return jax.shard_map(local, mesh=mesh, in_specs=in_specs, out_specs=out_specs, check_vma=False)
```

```python
import functools

import jax
import jax.numpy as jnp
from jax import lax
from jax.experimental import pallas as pl
from jax.experimental.pallas import tpu as pltpu
from jax.sharding import PartitionSpec as P

REACH = 12
CAP = 2
MESH = pl.DeviceIdType.MESH
EXACT = lax.Precision.HIGHEST


def split(value):
    high = value.astype(jnp.bfloat16)
    return high, (value - high.astype(jnp.float32)).astype(jnp.bfloat16)


def split_dot(left, right_pair):
    rows, cols = left.shape[0], right_pair.shape[1] // 2
    both = jnp.dot(
        jnp.concatenate(split(left), axis=0), right_pair, preferred_element_type=jnp.float32)
    return both[:rows, :cols] + (both[:rows, cols:] + both[rows:, :cols])


def exchange(
    mem, lev,
    holder_ref, table_ref, bg_hbm, map_hbm, sensed_hbm, precision_hbm,
    pw_ref, st_ref, scale_ref,
    bg_ref, map_ref, sensed_ref, precision_ref, local_sem,
    half, outgoing, part, arrived, pairs,
    part_send, part_recv, state_send, state_recv, z_send, z_recv, x_send, x_recv,
    y_send, y_recv, core_send, core_recv,
):
    me, lv = lax.axis_index("mem"), lax.axis_index("lev")
    blocks, members = half.shape[0], half.shape[1]
    layers = map_ref.shape[0]
    rows = members // lev
    mem_peers = [lax.rem(me + d, mem) for d in range(1, mem)]
    lev_peers = [lax.rem(lv + d, lev) for d in range(1, lev)]
    core = lv + 1 - 2 * lax.rem(lv, 2)
    across = lax.rem(lv + 2, lev)
    other = lax.rem(core + 2, lev)
    depth = mem // 2
    x = lax.rem(me, 2)
    side = me + 1 - 2 * x

    barrier = pltpu.get_barrier_semaphore()
    for k in mem_peers:
        pl.semaphore_signal(barrier, inc=1, device_id=(k, lv), device_id_type=MESH)
    for k in lev_peers:
        pl.semaphore_signal(barrier, inc=1, device_id=(me, k), device_id_type=MESH)

    loads = []
    for i, (src, dst) in enumerate((
            (map_hbm, map_ref), (bg_hbm, bg_ref),
            (sensed_hbm, sensed_ref), (precision_hbm, precision_ref))):
        c = pltpu.make_async_copy(src, dst, local_sem.at[i])
        c.start()
        loads.append(c)

    holder = [holder_ref[b] for b in range(blocks)]
    order = [
        sum(((holder[e] == holder[b]).astype(jnp.int32) for e in range(b)), jnp.int32(0))
        for b in range(blocks)]
    slot_of = [holder[b] * CAP + order[b] for b in range(blocks)]

    def find(slot):
        tile, live = jnp.int32(0), jnp.int32(0)
        for b in range(blocks):
            hit = slot_of[b] == slot
            tile = jnp.where(hit, b, tile)
            live = jnp.where(hit, 1, live)
        return tile, live.astype(jnp.float32)

    loads[0].wait()
    loads[1].wait()
    table_pair = jnp.concatenate(
        [jnp.concatenate(split(map_ref[h]), axis=1) for h in range(layers)], axis=0)
    for b in range(blocks):
        state = jnp.concatenate([
            bg_ref[pl.ds(b * layers + h, members, stride=blocks * layers), :]
            for h in range(layers)], axis=1)
        half[b] = state.astype(jnp.bfloat16)
        total = split_dot(state, table_pair)
        for q in range(lev):
            part[q, b] = total[q * rows:(q + 1) * rows]

    pl.semaphore_wait(barrier, mem - 1 + lev - 1)

    copies = []
    part_copies = []
    for d in range(1, lev):
        to = lev_peers[d - 1]
        c = pltpu.make_async_remote_copy(
            part.at[to], arrived.at[d], part_send.at[d], part_recv.at[d],
            device_id=(me, to), device_id_type=MESH)
        c.start()
        part_copies.append(c)

    def send_states(distances):
        for d in distances:
            to = mem_peers[d - 1]
            for c in range(CAP):
                tile, live = find(to * CAP + c)
                outgoing[d, c] = half[tile] * live.astype(jnp.bfloat16)
            copy = pltpu.make_async_remote_copy(
                outgoing.at[d], st_ref.at[me], state_send.at[d], state_recv.at[d],
                device_id=(to, lv), device_id_type=MESH)
            copy.start()
            copies.append(copy)

    early = [d for d in range(1, mem) if d in (depth, depth + 1)]
    send_states(early)
    for c in range(CAP):
        tile, live = find(me * CAP + c)
        st_ref[me, c] = half[tile] * live.astype(jnp.bfloat16)

    loads[2].wait()
    loads[3].wait()
    for b in range(blocks):
        pairs[b] = jnp.concatenate(split(precision_ref[b]), axis=1)
    for c in part_copies:
        c.wait_recv()
    for b in range(blocks):
        pred = part[lv, b]
        for d in range(1, lev):
            pred = pred + arrived[d, b]
        pw_ref[me, lv, 0, b] = pred.astype(jnp.bfloat16)
        gap = sensed_ref[pl.ds(lv * rows * blocks + b, rows, stride=blocks), :] - pred
        pw_ref[me, lv, 1, b] = split_dot(gap, pairs[b]).astype(jnp.bfloat16)

    def pass_on(owner, quarter, send, recv, to):
        return pltpu.make_async_remote_copy(
            pw_ref.at[owner, quarter], pw_ref.at[owner, quarter], send, recv,
            device_id=to, device_id_type=MESH)

    def begin(*args):
        c = pass_on(*args)
        c.start()
        copies.append(c)

    near = [lax.rem(me + mem - 2 * d, mem) for d in range(depth)]
    far = [lax.rem(side + mem - 2 * d, mem) for d in range(depth)]
    owners = near + far
    for d in range(1, depth):
        begin(me, lv, z_send.at[d], z_recv.at[d], (lax.rem(me + 2 * d, mem), lv))

    def spread(e):
        begin(owners[e], lv, y_send.at[e], y_recv.at[e], (me, across))
        begin(owners[e], lv, core_send.at[0, e], core_recv.at[0, e], (me, core))

    begin(me, lv, x_send.at[0], x_recv.at[0], (side, lv))
    spread(0)
    send_states([d for d in range(1, mem) if d not in early])
    pass_on(far[0], lv, x_send.at[0], x_recv.at[0], (side, lv)).wait_recv()
    spread(depth)
    for d in range(1, depth):
        pass_on(near[d], lv, z_send.at[d], z_recv.at[d], (near[d], lv)).wait_recv()
        begin(near[d], lv, x_send.at[d], x_recv.at[d], (side, lv))
        spread(d)
        pass_on(far[d], lv, x_send.at[d], x_recv.at[d], (side, lv)).wait_recv()
        spread(depth + d)

    here = [find(me * CAP + c) for c in range(CAP)]
    for c in range(CAP):
        tile, live = here[c]
        listed = [table_ref[tile, q] for q in range(table_ref.shape[1])]
        for b in range(blocks):
            times = sum(((entry == b).astype(jnp.int32) for entry in listed), jnp.int32(0))
            away = jnp.abs(tile - b)
            gap = jnp.minimum(away, blocks - away)
            weight = jnp.float32(0)
            for g in range(blocks // 2 + 1):
                value = 1.0 / (1.0 + (2.0 * g / REACH) ** 2) / (mem * members - 1)
                weight = jnp.where(gap == g, jnp.float32(value), weight)
            scale_ref[c * blocks + b] = times.astype(jnp.float32) * weight * live

    turns = [0, depth] + [e for d in range(1, depth) for e in (d, depth + d)]
    for e in turns:
        pass_on(owners[e], across, y_send.at[e], y_recv.at[e], (me, across)).wait_recv()
        begin(owners[e], across, core_send.at[1, e], core_recv.at[1, e], (me, core))
    for e in turns:
        pass_on(owners[e], core, core_send.at[0, e], core_recv.at[0, e], (me, core)).wait_recv()
        pass_on(owners[e], other, core_send.at[1, e], core_recv.at[1, e], (me, core)).wait_recv()
    for d in range(1, mem):
        source = lax.rem(me + mem - d, mem)
        pltpu.make_async_remote_copy(
            outgoing.at[d], st_ref.at[source], state_send.at[d], state_recv.at[d],
            device_id=(source, lv), device_id_type=MESH).wait_recv()
    for c in part_copies + copies:
        c.wait_send()


def analyse(scale_ref, pw_ref, st_ref, out_ref, covariance):
    mem, lev, _, blocks, rows, obs = pw_ref.shape
    capacity, members, width = st_ref.shape[1:]
    total = mem * members

    @pl.loop(0, blocks)
    def _(b):
        pred = pw_ref[:, :, 0, b].reshape(total, obs).astype(jnp.float32)
        mean = jnp.sum(pred, axis=0, keepdims=True) * (1.0 / total)
        pert = (pred - mean).astype(jnp.bfloat16)
        for c in range(capacity):
            cov = lax.dot_general(
                pert, st_ref[:, c].reshape(total, width), (((0,), (0,)), ((), ())),
                preferred_element_type=jnp.float32)
            covariance[pl.ds(pl.multiple_of(b * obs, obs), obs), c * width:(c + 1) * width] = (
                cov * scale_ref[c * blocks + b]).astype(jnp.bfloat16)

    parts = 4 if mem % 4 == 0 else mem
    chunk = mem // parts

    @pl.loop(0, parts)
    def _(r):
        owners = pl.ds(r * chunk, chunk)
        weighted = jnp.concatenate(
            [pw_ref[owners, :, 1, b].reshape(chunk * members, obs) for b in range(blocks)], axis=1)
        per_slot = width // 128
        for c in range(capacity):
            rise = jnp.dot(
                weighted, covariance[:, c * width:(c + 1) * width],
                preferred_element_type=jnp.float32)
            value = st_ref[owners, c].reshape(chunk * members, width).astype(jnp.float32) + rise
            for h in range(per_slot):
                stride = capacity * per_slot
                start = r * chunk * members * stride + c * per_slot + h
                out_ref[pl.ds(start, chunk * members, stride=stride), :] = (
                    value[:, h * 128:(h + 1) * 128])


def dense_shards(mem, lev, bg, linear_map, sensed, precision, table, holder_rank):
    members, blocks, layers, sites = bg.shape
    obs = linear_map.shape[2]
    rows = members // lev
    width = layers * sites
    smem = pl.BlockSpec(memory_space=pltpu.SMEM)
    vmem = pl.BlockSpec(memory_space=pltpu.VMEM)
    hbm = pl.BlockSpec(memory_space=pltpu.HBM)
    dma = pltpu.SemaphoreType.DMA
    half = jnp.bfloat16
    wide = jnp.float32
    pw, st, scale = pl.pallas_call(
        functools.partial(exchange, mem, lev),
        out_shape=(
            jax.ShapeDtypeStruct((mem, lev, 2, blocks, rows, obs), half),
            jax.ShapeDtypeStruct((mem, CAP, members, width), half),
            jax.ShapeDtypeStruct((CAP * blocks,), wide),
        ),
        in_specs=[smem, smem, hbm, hbm, hbm, hbm],
        out_specs=(vmem, vmem, smem),
        scratch_shapes=[
            pltpu.VMEM((members * blocks * layers, sites), wide),
            pltpu.VMEM(linear_map.shape, wide),
            pltpu.VMEM((members * blocks, obs), wide),
            pltpu.VMEM(precision.shape, wide),
            dma((4,)),
            pltpu.VMEM((blocks, members, width), half),
            pltpu.VMEM((mem, CAP, members, width), half),
            pltpu.VMEM((lev, blocks, rows, obs), wide),
            pltpu.VMEM((lev, blocks, rows, obs), wide),
            pltpu.VMEM((blocks, obs, 2 * obs), half),
            dma((lev,)), dma((lev,)), dma((mem,)), dma((mem,)),
            dma((mem,)), dma((mem,)), dma((mem,)), dma((mem,)),
            dma((mem,)), dma((mem,)), dma((2, mem)), dma((2, mem)),
        ],
        compiler_params=pltpu.CompilerParams(
            collective_id=0, has_side_effects=True, vmem_limit_bytes=40 * 2**20),
        name="exchange",
    )(
        holder_rank, table, bg.reshape(members * blocks * layers, sites), linear_map,
        sensed.reshape(members * blocks, obs), precision,
    )
    out = pl.pallas_call(
        analyse,
        out_shape=jax.ShapeDtypeStruct((mem * members * CAP * layers, sites), jnp.float32),
        in_specs=[smem, vmem, vmem],
        out_specs=vmem,
        scratch_shapes=[pltpu.VMEM((blocks * obs, CAP * width), half)],
        compiler_params=pltpu.CompilerParams(vmem_limit_bytes=40 * 2**20),
        name="analyse",
    )(scale, pw, st)
    return out.reshape(mem * members, CAP, layers, sites)


def shards(
    background_trajectories,
    linear_sensor_mapping,
    jittered_sensor_values,
    residual_precision_tiles,
    measurement_tile_table,
    holder_rank,
):
    largest_ordering_label = lax.Precision.HIGHEST
    mem_count = lax.axis_size("mem")
    my_index = lax.axis_index("mem")
    resident_realizations, tile_count, layer_count, mesh_sites = background_trajectories.shape
    obs_width = linear_sensor_mapping.shape[2]
    listed = measurement_tile_table.shape[1]
    capacity = CAP
    slot_count = mem_count * capacity
    partial_observed = jnp.einsum(
        "vhsg,sgl->vhl",
        background_trajectories,
        linear_sensor_mapping,
        precision=largest_ordering_label,
    )
    aggregated_total = lax.psum(partial_observed, "lev")
    departure = jittered_sensor_values - aggregated_total
    weighted = jnp.einsum(
        "mbo,bop->mbp", departure, residual_precision_tiles, precision=largest_ordering_label
    ).astype(jnp.bfloat16)
    background_values_mapped = aggregated_total.astype(jnp.bfloat16)
    blocks = jnp.arange(tile_count, dtype=jnp.int32)
    shared_owner = holder_rank[:, None] == holder_rank[None, :]
    earlier = blocks[None, :] < blocks[:, None]
    order_rank = jnp.sum((shared_owner & earlier).astype(jnp.int32), axis=1)
    slot_of_block = holder_rank * capacity + order_rank
    slot_ids = jnp.arange(slot_count, dtype=jnp.int32)
    matches = slot_of_block[None, :] == slot_ids[:, None]
    active_slot = jnp.any(matches, axis=1)
    tile_at_place = jnp.sum(jnp.where(matches, blocks[None, :], 0), axis=1)
    obs_index = jnp.take(measurement_tile_table, tile_at_place, axis=0)
    offsets_abs = jnp.abs(tile_at_place[:, None] - obs_index)
    cycle_gap = jnp.minimum(offsets_abs, tile_count - offsets_abs).astype(jnp.float32)
    scaled_gap = 2.0 * cycle_gap / REACH
    taper_weight = 1.0 / (1.0 + scaled_gap * scaled_gap)
    outgoing = (
        jnp.take(background_trajectories, tile_at_place, axis=1)
        * active_slot.astype(jnp.float32)[None, :, None, None]
    )
    outgoing = outgoing.reshape(
        resident_realizations, mem_count, capacity, layer_count * mesh_sites
    )
    states = lax.all_to_all(outgoing, "mem", split_axis=1, concat_axis=0, tiled=True).reshape(
        -1, capacity, layer_count * mesh_sites
    )
    total_members = states.shape[0]
    gathered = (
        lax.all_gather(background_values_mapped, "mem", axis=0, tiled=True),
        lax.all_gather(weighted, "mem", axis=0, tiled=True),
    )
    mine_index = lax.dynamic_slice_in_dim(obs_index, my_index * capacity, capacity, 0).reshape(-1)
    mine_live = lax.dynamic_slice_in_dim(active_slot, my_index * capacity, capacity, 0)
    mine_mask = jnp.repeat(mine_live, listed).astype(jnp.bfloat16)
    pred_rows = jnp.take(gathered[0], mine_index, axis=1) * mine_mask[None, :, None]
    weight_rows = jnp.take(gathered[1], mine_index, axis=1) * mine_mask[None, :, None]
    my_taper = lax.dynamic_slice_in_dim(taper_weight, my_index * capacity, capacity, 0)
    state_half = states.astype(jnp.bfloat16)
    mean_pred = jnp.mean(pred_rows, axis=0, dtype=jnp.float32)
    pred_pert = (
        (pred_rows - mean_pred)
        .astype(jnp.bfloat16)
        .reshape(total_members, capacity, listed * obs_width)
    )
    weight_cols = weight_rows.reshape(total_members, capacity, listed * obs_width)
    covariance = jnp.einsum(
        "mcx,mcy->cxy", state_half, pred_pert, preferred_element_type=jnp.float32
    )
    column_scale = jnp.repeat(my_taper, obs_width, axis=1) / (total_members - 1)
    covariance = (covariance * column_scale[:, None, :]).astype(jnp.bfloat16)
    increment = jnp.einsum(
        "mcy,cxy->mcx", weight_cols, covariance, preferred_element_type=jnp.float32
    )
    return (states + increment).reshape(total_members, capacity, layer_count, mesh_sites)


def solution(mesh):
    in_specs = (
        P("mem", None, "lev", None),
        P("lev", None, None),
        P("mem", None, None),
        P(),
        P(),
        P(),
    )
    out_specs = P(None, "mem", "lev", None)
    mem, lev = mesh.shape["mem"], mesh.shape["lev"]

    def local(bg, linear_map, sensed, precision, table, holder_rank):
        dense = bg.shape[1] <= table.shape[1] and lev == 4 and mem % 2 == 0 and bg.shape[0] % 64 == 0
        body = functools.partial(dense_shards, mem, lev) if dense else shards
        return body(bg, linear_map, sensed, precision, table, holder_rank)

    return jax.shard_map(local, mesh=mesh, in_specs=in_specs, out_specs=out_specs, check_vma=False)
```

```python
import functools

import jax
import jax.numpy as jnp
from jax import lax
from jax.experimental import pallas as pl
from jax.experimental.pallas import tpu as pltpu
from jax.sharding import PartitionSpec as P

REACH = 12
CAP = 2
MESH = pl.DeviceIdType.MESH
EXACT = lax.Precision.HIGHEST


def split(value):
    high = value.astype(jnp.bfloat16)
    return high, (value - high.astype(jnp.float32)).astype(jnp.bfloat16)


def split_dot(left, right_pair):
    rows, cols = left.shape[0], right_pair.shape[1] // 2
    both = jnp.dot(
        jnp.concatenate(split(left), axis=0), right_pair, preferred_element_type=jnp.float32)
    return both[:rows, :cols] + (both[:rows, cols:] + both[rows:, :cols])


def split_three(value):
    high = value.astype(jnp.bfloat16)
    rest = value - high.astype(jnp.float32)
    return (high,) + split(rest)


def exact_dot(left, right_three):
    rows, cols = left.shape[0], right_three.shape[1] // 3
    all_pairs = jnp.dot(
        jnp.concatenate(split_three(left), axis=0), right_three,
        preferred_element_type=jnp.float32)
    term = lambda i, k: all_pairs[i * rows:(i + 1) * rows, k * cols:(k + 1) * cols]
    small = term(0, 2) + term(1, 1) + term(2, 0)
    return term(0, 0) + ((term(0, 1) + term(1, 0)) + small)


def exchange(
    mem, lev,
    holder_ref, table_ref, bg_hbm, map_hbm, sensed_hbm, precision_hbm,
    pw_ref, st_ref, scale_ref,
    bg_ref, map_ref, sensed_ref, precision_ref, local_sem,
    half, outgoing, part, arrived, pairs,
    part_send, part_recv, state_send, state_recv, z_send, z_recv, x_send, x_recv,
    y_send, y_recv, core_send, core_recv,
):
    me, lv = lax.axis_index("mem"), lax.axis_index("lev")
    blocks, members = half.shape[0], half.shape[1]
    layers = map_ref.shape[0]
    rows = members // lev
    mem_peers = [lax.rem(me + d, mem) for d in range(1, mem)]
    lev_peers = [lax.rem(lv + d, lev) for d in range(1, lev)]
    core = lv + 1 - 2 * lax.rem(lv, 2)
    across = lax.rem(lv + 2, lev)
    other = lax.rem(core + 2, lev)
    depth = mem // 2
    x = lax.rem(me, 2)
    side = me + 1 - 2 * x

    barrier = pltpu.get_barrier_semaphore()
    for k in mem_peers:
        pl.semaphore_signal(barrier, inc=1, device_id=(k, lv), device_id_type=MESH)
    for k in lev_peers:
        pl.semaphore_signal(barrier, inc=1, device_id=(me, k), device_id_type=MESH)

    loads = []
    for i, (src, dst) in enumerate((
            (map_hbm, map_ref), (bg_hbm, bg_ref),
            (sensed_hbm, sensed_ref), (precision_hbm, precision_ref))):
        c = pltpu.make_async_copy(src, dst, local_sem.at[i])
        c.start()
        loads.append(c)

    holder = [holder_ref[b] for b in range(blocks)]
    order = [
        sum(((holder[e] == holder[b]).astype(jnp.int32) for e in range(b)), jnp.int32(0))
        for b in range(blocks)]
    slot_of = [holder[b] * CAP + order[b] for b in range(blocks)]

    def find(slot):
        tile, live = jnp.int32(0), jnp.int32(0)
        for b in range(blocks):
            hit = slot_of[b] == slot
            tile = jnp.where(hit, b, tile)
            live = jnp.where(hit, 1, live)
        return tile, live.astype(jnp.float32)

    loads[0].wait()
    loads[1].wait()
    map_three = jnp.concatenate(
        [jnp.concatenate(split_three(map_ref[h]), axis=1) for h in range(layers)], axis=0)
    for b in range(blocks):
        state = jnp.concatenate([
            bg_ref[pl.ds(b * layers + h, members, stride=blocks * layers), :]
            for h in range(layers)], axis=1)
        half[b] = state.astype(jnp.bfloat16)
        total = exact_dot(state, map_three)
        for q in range(lev):
            part[q, b] = total[q * rows:(q + 1) * rows]

    pl.semaphore_wait(barrier, mem - 1 + lev - 1)

    copies = []
    part_copies = []
    for d in range(1, lev):
        to = lev_peers[d - 1]
        c = pltpu.make_async_remote_copy(
            part.at[to], arrived.at[d], part_send.at[d], part_recv.at[d],
            device_id=(me, to), device_id_type=MESH)
        c.start()
        part_copies.append(c)

    def send_states(distances):
        for d in distances:
            to = mem_peers[d - 1]
            for c in range(CAP):
                tile, live = find(to * CAP + c)
                outgoing[d, c] = half[tile] * live.astype(jnp.bfloat16)
            copy = pltpu.make_async_remote_copy(
                outgoing.at[d], st_ref.at[me], state_send.at[d], state_recv.at[d],
                device_id=(to, lv), device_id_type=MESH)
            copy.start()
            copies.append(copy)

    for c in range(CAP):
        tile, live = find(me * CAP + c)
        st_ref[me, c] = half[tile] * live.astype(jnp.bfloat16)

    loads[2].wait()
    loads[3].wait()
    for b in range(blocks):
        pairs[b] = jnp.concatenate(split(precision_ref[b]), axis=1)
    for c in part_copies:
        c.wait_recv()
    for b in range(blocks):
        pred = part[lv, b]
        for d in range(1, lev):
            pred = pred + arrived[d, b]
        pw_ref[me, lv, 0, b] = pred.astype(jnp.bfloat16)
        gap = sensed_ref[pl.ds(lv * rows * blocks + b, rows, stride=blocks), :] - pred
        pw_ref[me, lv, 1, b] = split_dot(gap, pairs[b]).astype(jnp.bfloat16)

    def pass_on(owner, quarter, send, recv, to):
        return pltpu.make_async_remote_copy(
            pw_ref.at[owner, quarter], pw_ref.at[owner, quarter], send, recv,
            device_id=to, device_id_type=MESH)

    def begin(*args):
        c = pass_on(*args)
        c.start()
        copies.append(c)

    near = [lax.rem(me + mem - 2 * d, mem) for d in range(depth)]
    far = [lax.rem(side + mem - 2 * d, mem) for d in range(depth)]
    owners = near + far
    for d in range(1, depth):
        begin(me, lv, z_send.at[d], z_recv.at[d], (lax.rem(me + 2 * d, mem), lv))

    def spread(e):
        begin(owners[e], lv, y_send.at[e], y_recv.at[e], (me, across))
        begin(owners[e], lv, core_send.at[0, e], core_recv.at[0, e], (me, core))

    begin(me, lv, x_send.at[0], x_recv.at[0], (side, lv))
    spread(0)
    send_states(range(1, mem))
    pass_on(far[0], lv, x_send.at[0], x_recv.at[0], (side, lv)).wait_recv()
    spread(depth)
    for d in range(1, depth):
        pass_on(near[d], lv, z_send.at[d], z_recv.at[d], (near[d], lv)).wait_recv()
        begin(near[d], lv, x_send.at[d], x_recv.at[d], (side, lv))
        spread(d)
        pass_on(far[d], lv, x_send.at[d], x_recv.at[d], (side, lv)).wait_recv()
        spread(depth + d)

    here = [find(me * CAP + c) for c in range(CAP)]
    for c in range(CAP):
        tile, live = here[c]
        listed = [table_ref[tile, q] for q in range(table_ref.shape[1])]
        for b in range(blocks):
            times = sum(((entry == b).astype(jnp.int32) for entry in listed), jnp.int32(0))
            away = jnp.abs(tile - b)
            gap = jnp.minimum(away, blocks - away)
            weight = jnp.float32(0)
            for g in range(blocks // 2 + 1):
                value = 1.0 / (1.0 + (2.0 * g / REACH) ** 2) / (mem * members - 1)
                weight = jnp.where(gap == g, jnp.float32(value), weight)
            scale_ref[c * blocks + b] = times.astype(jnp.float32) * weight * live

    turns = [0, depth] + [e for d in range(1, depth) for e in (d, depth + d)]
    for e in turns:
        pass_on(owners[e], across, y_send.at[e], y_recv.at[e], (me, across)).wait_recv()
        begin(owners[e], across, core_send.at[1, e], core_recv.at[1, e], (me, core))
    for e in turns:
        pass_on(owners[e], core, core_send.at[0, e], core_recv.at[0, e], (me, core)).wait_recv()
        pass_on(owners[e], other, core_send.at[1, e], core_recv.at[1, e], (me, core)).wait_recv()
    for d in range(1, mem):
        source = lax.rem(me + mem - d, mem)
        pltpu.make_async_remote_copy(
            outgoing.at[d], st_ref.at[source], state_send.at[d], state_recv.at[d],
            device_id=(source, lv), device_id_type=MESH).wait_recv()
    for c in part_copies + copies:
        c.wait_send()


def analyse(scale_ref, pw_ref, st_ref, out_ref, covariance):
    mem, lev, _, blocks, rows, obs = pw_ref.shape
    capacity, members, width = st_ref.shape[1:]
    total = mem * members

    @pl.loop(0, blocks)
    def _(b):
        pred = pw_ref[:, :, 0, b].reshape(total, obs).astype(jnp.float32)
        mean = jnp.sum(pred, axis=0, keepdims=True) * (1.0 / total)
        pert = (pred - mean).astype(jnp.bfloat16)
        for c in range(capacity):
            cov = lax.dot_general(
                pert, st_ref[:, c].reshape(total, width), (((0,), (0,)), ((), ())),
                preferred_element_type=jnp.float32)
            covariance[pl.ds(pl.multiple_of(b * obs, obs), obs), c * width:(c + 1) * width] = (
                cov * scale_ref[c * blocks + b]).astype(jnp.bfloat16)

    parts = 4 if mem % 4 == 0 else mem
    chunk = mem // parts

    @pl.loop(0, parts)
    def _(r):
        owners = pl.ds(r * chunk, chunk)
        weighted = jnp.concatenate(
            [pw_ref[owners, :, 1, b].reshape(chunk * members, obs) for b in range(blocks)], axis=1)
        per_slot = width // 128
        for c in range(capacity):
            rise = jnp.dot(
                weighted, covariance[:, c * width:(c + 1) * width],
                preferred_element_type=jnp.float32)
            value = st_ref[owners, c].reshape(chunk * members, width).astype(jnp.float32) + rise
            for h in range(per_slot):
                stride = capacity * per_slot
                start = r * chunk * members * stride + c * per_slot + h
                out_ref[pl.ds(start, chunk * members, stride=stride), :] = (
                    value[:, h * 128:(h + 1) * 128])


def dense_shards(mem, lev, bg, linear_map, sensed, precision, table, holder_rank):
    members, blocks, layers, sites = bg.shape
    obs = linear_map.shape[2]
    rows = members // lev
    width = layers * sites
    smem = pl.BlockSpec(memory_space=pltpu.SMEM)
    vmem = pl.BlockSpec(memory_space=pltpu.VMEM)
    hbm = pl.BlockSpec(memory_space=pltpu.HBM)
    dma = pltpu.SemaphoreType.DMA
    half = jnp.bfloat16
    wide = jnp.float32
    pw, st, scale = pl.pallas_call(
        functools.partial(exchange, mem, lev),
        out_shape=(
            jax.ShapeDtypeStruct((mem, lev, 2, blocks, rows, obs), half),
            jax.ShapeDtypeStruct((mem, CAP, members, width), half),
            jax.ShapeDtypeStruct((CAP * blocks,), wide),
        ),
        in_specs=[smem, smem, hbm, hbm, hbm, hbm],
        out_specs=(vmem, vmem, smem),
        scratch_shapes=[
            pltpu.VMEM((members * blocks * layers, sites), wide),
            pltpu.VMEM(linear_map.shape, wide),
            pltpu.VMEM((members * blocks, obs), wide),
            pltpu.VMEM(precision.shape, wide),
            dma((4,)),
            pltpu.VMEM((blocks, members, width), half),
            pltpu.VMEM((mem, CAP, members, width), half),
            pltpu.VMEM((lev, blocks, rows, obs), wide),
            pltpu.VMEM((lev, blocks, rows, obs), wide),
            pltpu.VMEM((blocks, obs, 2 * obs), half),
            dma((lev,)), dma((lev,)), dma((mem,)), dma((mem,)),
            dma((mem,)), dma((mem,)), dma((mem,)), dma((mem,)),
            dma((mem,)), dma((mem,)), dma((2, mem)), dma((2, mem)),
        ],
        compiler_params=pltpu.CompilerParams(
            collective_id=0, has_side_effects=True, vmem_limit_bytes=40 * 2**20),
        name="exchange",
    )(
        holder_rank, table, bg.reshape(members * blocks * layers, sites), linear_map,
        sensed.reshape(members * blocks, obs), precision,
    )
    out = pl.pallas_call(
        analyse,
        out_shape=jax.ShapeDtypeStruct((mem * members * CAP * layers, sites), jnp.float32),
        in_specs=[smem, vmem, vmem],
        out_specs=vmem,
        scratch_shapes=[pltpu.VMEM((blocks * obs, CAP * width), half)],
        compiler_params=pltpu.CompilerParams(vmem_limit_bytes=40 * 2**20),
        name="analyse",
    )(scale, pw, st)
    return out.reshape(mem * members, CAP, layers, sites)


def shards(
    background_trajectories,
    linear_sensor_mapping,
    jittered_sensor_values,
    residual_precision_tiles,
    measurement_tile_table,
    holder_rank,
):
    largest_ordering_label = lax.Precision.HIGHEST
    mem_count = lax.axis_size("mem")
    my_index = lax.axis_index("mem")
    resident_realizations, tile_count, layer_count, mesh_sites = background_trajectories.shape
    obs_width = linear_sensor_mapping.shape[2]
    listed = measurement_tile_table.shape[1]
    capacity = CAP
    slot_count = mem_count * capacity
    partial_observed = jnp.einsum(
        "vhsg,sgl->vhl",
        background_trajectories,
        linear_sensor_mapping,
        precision=largest_ordering_label,
    )
    aggregated_total = lax.psum(partial_observed, "lev")
    departure = jittered_sensor_values - aggregated_total
    weighted = jnp.einsum(
        "mbo,bop->mbp", departure, residual_precision_tiles, precision=largest_ordering_label
    ).astype(jnp.bfloat16)
    background_values_mapped = aggregated_total.astype(jnp.bfloat16)
    blocks = jnp.arange(tile_count, dtype=jnp.int32)
    shared_owner = holder_rank[:, None] == holder_rank[None, :]
    earlier = blocks[None, :] < blocks[:, None]
    order_rank = jnp.sum((shared_owner & earlier).astype(jnp.int32), axis=1)
    slot_of_block = holder_rank * capacity + order_rank
    slot_ids = jnp.arange(slot_count, dtype=jnp.int32)
    matches = slot_of_block[None, :] == slot_ids[:, None]
    active_slot = jnp.any(matches, axis=1)
    tile_at_place = jnp.sum(jnp.where(matches, blocks[None, :], 0), axis=1)
    obs_index = jnp.take(measurement_tile_table, tile_at_place, axis=0)
    offsets_abs = jnp.abs(tile_at_place[:, None] - obs_index)
    cycle_gap = jnp.minimum(offsets_abs, tile_count - offsets_abs).astype(jnp.float32)
    scaled_gap = 2.0 * cycle_gap / REACH
    taper_weight = 1.0 / (1.0 + scaled_gap * scaled_gap)
    outgoing = (
        jnp.take(background_trajectories, tile_at_place, axis=1)
        * active_slot.astype(jnp.float32)[None, :, None, None]
    )
    outgoing = outgoing.reshape(
        resident_realizations, mem_count, capacity, layer_count * mesh_sites
    )
    states = lax.all_to_all(outgoing, "mem", split_axis=1, concat_axis=0, tiled=True).reshape(
        -1, capacity, layer_count * mesh_sites
    )
    total_members = states.shape[0]
    gathered = (
        lax.all_gather(background_values_mapped, "mem", axis=0, tiled=True),
        lax.all_gather(weighted, "mem", axis=0, tiled=True),
    )
    mine_index = lax.dynamic_slice_in_dim(obs_index, my_index * capacity, capacity, 0).reshape(-1)
    mine_live = lax.dynamic_slice_in_dim(active_slot, my_index * capacity, capacity, 0)
    mine_mask = jnp.repeat(mine_live, listed).astype(jnp.bfloat16)
    pred_rows = jnp.take(gathered[0], mine_index, axis=1) * mine_mask[None, :, None]
    weight_rows = jnp.take(gathered[1], mine_index, axis=1) * mine_mask[None, :, None]
    my_taper = lax.dynamic_slice_in_dim(taper_weight, my_index * capacity, capacity, 0)
    state_half = states.astype(jnp.bfloat16)
    mean_pred = jnp.mean(pred_rows, axis=0, dtype=jnp.float32)
    pred_pert = (
        (pred_rows - mean_pred)
        .astype(jnp.bfloat16)
        .reshape(total_members, capacity, listed * obs_width)
    )
    weight_cols = weight_rows.reshape(total_members, capacity, listed * obs_width)
    covariance = jnp.einsum(
        "mcx,mcy->cxy", state_half, pred_pert, preferred_element_type=jnp.float32
    )
    column_scale = jnp.repeat(my_taper, obs_width, axis=1) / (total_members - 1)
    covariance = (covariance * column_scale[:, None, :]).astype(jnp.bfloat16)
    increment = jnp.einsum(
        "mcy,cxy->mcx", weight_cols, covariance, preferred_element_type=jnp.float32
    )
    return (states + increment).reshape(total_members, capacity, layer_count, mesh_sites)


def solution(mesh):
    in_specs = (
        P("mem", None, "lev", None),
        P("lev", None, None),
        P("mem", None, None),
        P(),
        P(),
        P(),
    )
    out_specs = P(None, "mem", "lev", None)
    mem, lev = mesh.shape["mem"], mesh.shape["lev"]

    def local(bg, linear_map, sensed, precision, table, holder_rank):
        dense = bg.shape[1] <= table.shape[1] and lev == 4 and mem % 2 == 0 and bg.shape[0] % 64 == 0
        body = functools.partial(dense_shards, mem, lev) if dense else shards
        return body(bg, linear_map, sensed, precision, table, holder_rank)

    return jax.shard_map(local, mesh=mesh, in_specs=in_specs, out_specs=out_specs, check_vma=False)
```

```python
import functools

import jax
import jax.numpy as jnp
from jax import lax
from jax.experimental import pallas as pl
from jax.experimental.pallas import tpu as pltpu
from jax.sharding import PartitionSpec as P

REACH = 12
CAP = 2
MESH = pl.DeviceIdType.MESH
EXACT = lax.Precision.HIGHEST


def split(value):
    high = value.astype(jnp.bfloat16)
    return high, (value - high.astype(jnp.float32)).astype(jnp.bfloat16)


def split_dot(left, right_pair):
    rows, cols = left.shape[0], right_pair.shape[1] // 2
    both = jnp.dot(
        jnp.concatenate(split(left), axis=0), right_pair, preferred_element_type=jnp.float32)
    return both[:rows, :cols] + (both[:rows, cols:] + both[rows:, :cols])


def split_three(value):
    high = value.astype(jnp.bfloat16)
    rest = value - high.astype(jnp.float32)
    return (high,) + split(rest)


def exact_dot(left, right_three):
    rows, cols = left.shape[0], right_three.shape[1] // 3
    all_pairs = jnp.dot(
        jnp.concatenate(split_three(left), axis=0), right_three,
        preferred_element_type=jnp.float32)
    term = lambda i, k: all_pairs[i * rows:(i + 1) * rows, k * cols:(k + 1) * cols]
    small = term(0, 2) + term(1, 1) + term(2, 0)
    return term(0, 0) + ((term(0, 1) + term(1, 0)) + small)


def exchange(
    mem, lev,
    holder_ref, table_ref, bg_hbm, map_hbm, sensed_hbm, precision_hbm,
    out_hbm,
    pw_ref, st_ref, scale_ref, out_ref, covariance, out_sem,
    bg_ref, map_ref, sensed_ref, precision_ref, local_sem,
    half, outgoing, part, arrived, pairs,
    part_send, part_recv, state_send, state_recv, z_send, z_recv, x_send, x_recv,
    y_send, y_recv, core_send, core_recv,
):
    me, lv = lax.axis_index("mem"), lax.axis_index("lev")
    blocks, members = half.shape[0], half.shape[1]
    layers = map_ref.shape[0]
    rows = members // lev
    mem_peers = [lax.rem(me + d, mem) for d in range(1, mem)]
    lev_peers = [lax.rem(lv + d, lev) for d in range(1, lev)]
    core = lv + 1 - 2 * lax.rem(lv, 2)
    across = lax.rem(lv + 2, lev)
    other = lax.rem(core + 2, lev)
    depth = mem // 2
    x = lax.rem(me, 2)
    side = me + 1 - 2 * x

    barrier = pltpu.get_barrier_semaphore()
    for k in mem_peers:
        pl.semaphore_signal(barrier, inc=1, device_id=(k, lv), device_id_type=MESH)
    for k in lev_peers:
        pl.semaphore_signal(barrier, inc=1, device_id=(me, k), device_id_type=MESH)

    loads = []
    for i, (src, dst) in enumerate((
            (map_hbm, map_ref), (bg_hbm, bg_ref),
            (sensed_hbm, sensed_ref), (precision_hbm, precision_ref))):
        c = pltpu.make_async_copy(src, dst, local_sem.at[i])
        c.start()
        loads.append(c)

    holder = [holder_ref[b] for b in range(blocks)]
    order = [
        sum(((holder[e] == holder[b]).astype(jnp.int32) for e in range(b)), jnp.int32(0))
        for b in range(blocks)]
    slot_of = [holder[b] * CAP + order[b] for b in range(blocks)]

    def find(slot):
        tile, live = jnp.int32(0), jnp.int32(0)
        for b in range(blocks):
            hit = slot_of[b] == slot
            tile = jnp.where(hit, b, tile)
            live = jnp.where(hit, 1, live)
        return tile, live.astype(jnp.float32)

    loads[0].wait()
    loads[1].wait()
    map_three = jnp.concatenate(
        [jnp.concatenate(split_three(map_ref[h]), axis=1) for h in range(layers)], axis=0)
    for b in range(blocks):
        state = jnp.concatenate([
            bg_ref[pl.ds(b * layers + h, members, stride=blocks * layers), :]
            for h in range(layers)], axis=1)
        half[b] = state.astype(jnp.bfloat16)
        total = exact_dot(state, map_three)
        for q in range(lev):
            part[q, b] = total[q * rows:(q + 1) * rows]

    pl.semaphore_wait(barrier, mem - 1 + lev - 1)

    copies = []
    part_copies = []
    for d in range(1, lev):
        to = lev_peers[d - 1]
        c = pltpu.make_async_remote_copy(
            part.at[to], arrived.at[d], part_send.at[d], part_recv.at[d],
            device_id=(me, to), device_id_type=MESH)
        c.start()
        part_copies.append(c)

    def send_states(distances):
        for d in distances:
            to = mem_peers[d - 1]
            for c in range(CAP):
                tile, live = find(to * CAP + c)
                outgoing[d, c] = half[tile] * live.astype(jnp.bfloat16)
            copy = pltpu.make_async_remote_copy(
                outgoing.at[d], st_ref.at[me], state_send.at[d], state_recv.at[d],
                device_id=(to, lv), device_id_type=MESH)
            copy.start()
            copies.append(copy)

    for c in range(CAP):
        tile, live = find(me * CAP + c)
        st_ref[me, c] = half[tile] * live.astype(jnp.bfloat16)

    loads[2].wait()
    loads[3].wait()
    for b in range(blocks):
        pairs[b] = jnp.concatenate(split(precision_ref[b]), axis=1)
    for c in part_copies:
        c.wait_recv()
    for b in range(blocks):
        pred = part[lv, b]
        for d in range(1, lev):
            pred = pred + arrived[d, b]
        pw_ref[me, lv, 0, b] = pred.astype(jnp.bfloat16)
        gap = sensed_ref[pl.ds(lv * rows * blocks + b, rows, stride=blocks), :] - pred
        pw_ref[me, lv, 1, b] = split_dot(gap, pairs[b]).astype(jnp.bfloat16)

    def pass_on(owner, quarter, send, recv, to):
        return pltpu.make_async_remote_copy(
            pw_ref.at[owner, quarter], pw_ref.at[owner, quarter], send, recv,
            device_id=to, device_id_type=MESH)

    def begin(*args):
        c = pass_on(*args)
        c.start()
        copies.append(c)

    near = [lax.rem(me + mem - 2 * d, mem) for d in range(depth)]
    far = [lax.rem(side + mem - 2 * d, mem) for d in range(depth)]
    owners = near + far
    for d in range(1, depth):
        begin(me, lv, z_send.at[d], z_recv.at[d], (lax.rem(me + 2 * d, mem), lv))

    def spread(e):
        begin(owners[e], lv, y_send.at[e], y_recv.at[e], (me, across))
        begin(owners[e], lv, core_send.at[0, e], core_recv.at[0, e], (me, core))

    begin(me, lv, x_send.at[0], x_recv.at[0], (side, lv))
    spread(0)
    send_states(range(1, mem))
    pass_on(far[0], lv, x_send.at[0], x_recv.at[0], (side, lv)).wait_recv()
    spread(depth)
    for d in range(1, depth):
        pass_on(near[d], lv, z_send.at[d], z_recv.at[d], (near[d], lv)).wait_recv()
        begin(near[d], lv, x_send.at[d], x_recv.at[d], (side, lv))
        spread(d)
        pass_on(far[d], lv, x_send.at[d], x_recv.at[d], (side, lv)).wait_recv()
        spread(depth + d)

    here = [find(me * CAP + c) for c in range(CAP)]
    for c in range(CAP):
        tile, live = here[c]
        listed = [table_ref[tile, q] for q in range(table_ref.shape[1])]
        for b in range(blocks):
            times = sum(((entry == b).astype(jnp.int32) for entry in listed), jnp.int32(0))
            away = jnp.abs(tile - b)
            gap = jnp.minimum(away, blocks - away)
            weight = jnp.float32(0)
            for g in range(blocks // 2 + 1):
                value = 1.0 / (1.0 + (2.0 * g / REACH) ** 2) / (mem * members - 1)
                weight = jnp.where(gap == g, jnp.float32(value), weight)
            scale_ref[c * blocks + b] = times.astype(jnp.float32) * weight * live

    turns = [0, depth] + [e for d in range(1, depth) for e in (d, depth + d)]
    for e in turns:
        pass_on(owners[e], across, y_send.at[e], y_recv.at[e], (me, across)).wait_recv()
        begin(owners[e], across, core_send.at[1, e], core_recv.at[1, e], (me, core))
    for e in turns:
        pass_on(owners[e], core, core_send.at[0, e], core_recv.at[0, e], (me, core)).wait_recv()
        pass_on(owners[e], other, core_send.at[1, e], core_recv.at[1, e], (me, core)).wait_recv()
    for d in range(1, mem):
        source = lax.rem(me + mem - d, mem)
        pltpu.make_async_remote_copy(
            outgoing.at[d], st_ref.at[source], state_send.at[d], state_recv.at[d],
            device_id=(source, lv), device_id_type=MESH).wait_recv()
    analyse(scale_ref, pw_ref, st_ref, out_ref, out_hbm, covariance, out_sem)
    for c in part_copies + copies:
        c.wait_send()


def analyse(scale_ref, pw_ref, st_ref, out_ref, out_hbm, covariance, out_sem):
    mem, lev, _, blocks, rows, obs = pw_ref.shape
    capacity, members, width = st_ref.shape[1:]
    total = mem * members

    @pl.loop(0, blocks)
    def _(b):
        pred = pw_ref[:, :, 0, b].reshape(total, obs).astype(jnp.float32)
        mean = jnp.sum(pred, axis=0, keepdims=True) * (1.0 / total)
        pert = (pred - mean).astype(jnp.bfloat16)
        for c in range(capacity):
            cov = lax.dot_general(
                pert, st_ref[:, c].reshape(total, width), (((0,), (0,)), ((), ())),
                preferred_element_type=jnp.float32)
            covariance[pl.ds(pl.multiple_of(b * obs, obs), obs), c * width:(c + 1) * width] = (
                cov * scale_ref[c * blocks + b]).astype(jnp.bfloat16)

    parts = 2
    chunk = mem // parts
    stores = []
    for r in range(parts):
        owners = pl.ds(r * chunk, chunk)
        weighted = jnp.concatenate(
            [pw_ref[owners, :, 1, b].reshape(chunk * members, obs) for b in range(blocks)], axis=1)
        per_slot = width // 128
        stride = capacity * per_slot
        for c in range(capacity):
            rise = jnp.dot(
                weighted, covariance[:, c * width:(c + 1) * width],
                preferred_element_type=jnp.float32)
            value = st_ref[owners, c].reshape(chunk * members, width).astype(jnp.float32) + rise
            for h in range(per_slot):
                start = r * chunk * members * stride + c * per_slot + h
                out_ref[pl.ds(start, chunk * members, stride=stride), :] = (
                    value[:, h * 128:(h + 1) * 128])
        whole = pl.ds(r * chunk * members * stride, chunk * members * stride)
        store = pltpu.make_async_copy(out_ref.at[whole], out_hbm.at[whole], out_sem.at[r])
        store.start()
        stores.append(store)
    for store in stores:
        store.wait()


def dense_shards(mem, lev, bg, linear_map, sensed, precision, table, holder_rank):
    members, blocks, layers, sites = bg.shape
    obs = linear_map.shape[2]
    rows = members // lev
    width = layers * sites
    smem = pl.BlockSpec(memory_space=pltpu.SMEM)
    hbm = pl.BlockSpec(memory_space=pltpu.HBM)
    dma = pltpu.SemaphoreType.DMA
    half = jnp.bfloat16
    wide = jnp.float32
    out = pl.pallas_call(
        functools.partial(exchange, mem, lev),
        out_shape=jax.ShapeDtypeStruct((mem * members * CAP * layers, sites), wide),
        in_specs=[smem, smem, hbm, hbm, hbm, hbm],
        out_specs=hbm,
        scratch_shapes=[
            pltpu.VMEM((mem, lev, 2, blocks, rows, obs), half),
            pltpu.VMEM((mem, CAP, members, width), half),
            pltpu.SMEM((CAP * blocks,), wide),
            pltpu.VMEM((mem * members * CAP * layers, sites), wide),
            pltpu.VMEM((blocks * obs, CAP * width), half),
            dma((2,)),
            pltpu.VMEM((members * blocks * layers, sites), wide),
            pltpu.VMEM(linear_map.shape, wide),
            pltpu.VMEM((members * blocks, obs), wide),
            pltpu.VMEM(precision.shape, wide),
            dma((4,)),
            pltpu.VMEM((blocks, members, width), half),
            pltpu.VMEM((mem, CAP, members, width), half),
            pltpu.VMEM((lev, blocks, rows, obs), wide),
            pltpu.VMEM((lev, blocks, rows, obs), wide),
            pltpu.VMEM((blocks, obs, 2 * obs), half),
            dma((lev,)), dma((lev,)), dma((mem,)), dma((mem,)),
            dma((mem,)), dma((mem,)), dma((mem,)), dma((mem,)),
            dma((mem,)), dma((mem,)), dma((2, mem)), dma((2, mem)),
        ],
        compiler_params=pltpu.CompilerParams(
            collective_id=0, has_side_effects=True, vmem_limit_bytes=60 * 2**20),
        name="exchange",
    )(
        holder_rank, table, bg.reshape(members * blocks * layers, sites), linear_map,
        sensed.reshape(members * blocks, obs), precision,
    )
    return out.reshape(mem * members, CAP, layers, sites)


def shards(
    background_trajectories,
    linear_sensor_mapping,
    jittered_sensor_values,
    residual_precision_tiles,
    measurement_tile_table,
    holder_rank,
):
    largest_ordering_label = lax.Precision.HIGHEST
    mem_count = lax.axis_size("mem")
    my_index = lax.axis_index("mem")
    resident_realizations, tile_count, layer_count, mesh_sites = background_trajectories.shape
    obs_width = linear_sensor_mapping.shape[2]
    listed = measurement_tile_table.shape[1]
    capacity = CAP
    slot_count = mem_count * capacity
    partial_observed = jnp.einsum(
        "vhsg,sgl->vhl",
        background_trajectories,
        linear_sensor_mapping,
        precision=largest_ordering_label,
    )
    aggregated_total = lax.psum(partial_observed, "lev")
    departure = jittered_sensor_values - aggregated_total
    weighted = jnp.einsum(
        "mbo,bop->mbp", departure, residual_precision_tiles, precision=largest_ordering_label
    ).astype(jnp.bfloat16)
    background_values_mapped = aggregated_total.astype(jnp.bfloat16)
    blocks = jnp.arange(tile_count, dtype=jnp.int32)
    shared_owner = holder_rank[:, None] == holder_rank[None, :]
    earlier = blocks[None, :] < blocks[:, None]
    order_rank = jnp.sum((shared_owner & earlier).astype(jnp.int32), axis=1)
    slot_of_block = holder_rank * capacity + order_rank
    slot_ids = jnp.arange(slot_count, dtype=jnp.int32)
    matches = slot_of_block[None, :] == slot_ids[:, None]
    active_slot = jnp.any(matches, axis=1)
    tile_at_place = jnp.sum(jnp.where(matches, blocks[None, :], 0), axis=1)
    obs_index = jnp.take(measurement_tile_table, tile_at_place, axis=0)
    offsets_abs = jnp.abs(tile_at_place[:, None] - obs_index)
    cycle_gap = jnp.minimum(offsets_abs, tile_count - offsets_abs).astype(jnp.float32)
    scaled_gap = 2.0 * cycle_gap / REACH
    taper_weight = 1.0 / (1.0 + scaled_gap * scaled_gap)
    outgoing = (
        jnp.take(background_trajectories, tile_at_place, axis=1)
        * active_slot.astype(jnp.float32)[None, :, None, None]
    )
    outgoing = outgoing.reshape(
        resident_realizations, mem_count, capacity, layer_count * mesh_sites
    )
    states = lax.all_to_all(outgoing, "mem", split_axis=1, concat_axis=0, tiled=True).reshape(
        -1, capacity, layer_count * mesh_sites
    )
    total_members = states.shape[0]
    gathered = (
        lax.all_gather(background_values_mapped, "mem", axis=0, tiled=True),
        lax.all_gather(weighted, "mem", axis=0, tiled=True),
    )
    mine_index = lax.dynamic_slice_in_dim(obs_index, my_index * capacity, capacity, 0).reshape(-1)
    mine_live = lax.dynamic_slice_in_dim(active_slot, my_index * capacity, capacity, 0)
    mine_mask = jnp.repeat(mine_live, listed).astype(jnp.bfloat16)
    pred_rows = jnp.take(gathered[0], mine_index, axis=1) * mine_mask[None, :, None]
    weight_rows = jnp.take(gathered[1], mine_index, axis=1) * mine_mask[None, :, None]
    my_taper = lax.dynamic_slice_in_dim(taper_weight, my_index * capacity, capacity, 0)
    state_half = states.astype(jnp.bfloat16)
    mean_pred = jnp.mean(pred_rows, axis=0, dtype=jnp.float32)
    pred_pert = (
        (pred_rows - mean_pred)
        .astype(jnp.bfloat16)
        .reshape(total_members, capacity, listed * obs_width)
    )
    weight_cols = weight_rows.reshape(total_members, capacity, listed * obs_width)
    covariance = jnp.einsum(
        "mcx,mcy->cxy", state_half, pred_pert, preferred_element_type=jnp.float32
    )
    column_scale = jnp.repeat(my_taper, obs_width, axis=1) / (total_members - 1)
    covariance = (covariance * column_scale[:, None, :]).astype(jnp.bfloat16)
    increment = jnp.einsum(
        "mcy,cxy->mcx", weight_cols, covariance, preferred_element_type=jnp.float32
    )
    return (states + increment).reshape(total_members, capacity, layer_count, mesh_sites)


def solution(mesh):
    in_specs = (
        P("mem", None, "lev", None),
        P("lev", None, None),
        P("mem", None, None),
        P(),
        P(),
        P(),
    )
    out_specs = P(None, "mem", "lev", None)
    mem, lev = mesh.shape["mem"], mesh.shape["lev"]

    def local(bg, linear_map, sensed, precision, table, holder_rank):
        dense = bg.shape[1] <= table.shape[1] and lev == 4 and mem % 2 == 0 and bg.shape[0] % 64 == 0
        body = functools.partial(dense_shards, mem, lev) if dense else shards
        return body(bg, linear_map, sensed, precision, table, holder_rank)

    return jax.shard_map(local, mesh=mesh, in_specs=in_specs, out_specs=out_specs, check_vma=False)
```
